32 devices in a mesh: grid: 2 (over y), row: 4 (over x, core), col: 4 (over z).
Axes of the slice: x: 2, y: 2, z: 4, core: 2. Of those that a mesh axis runs over, the one named last changes fastest.
Arguments:
- schur: bfloat16 [2, 4096, 4096], P('grid', 'row', 'col'), may hold values from -6 to 6
- d_inv: bfloat16 [1, 2, 1024, 1024], P(None, 'grid', None, 'col'), may hold values from -0.0009765625 to 0.0087890625, as said below
- blocks: int32 [1, 2, 12], P(None, 'grid'), may hold values from 0 to 15, as said below
Outputs:
- merged: bfloat16 [2, 2048, 4096], P('grid', 'row', 'col')
The draws below stay inside these ranges and needn't reach their ends.
Inputs may be any that keep to these rules, and one draw needn't show every extreme that they name: blocks[l, g] is the same for all grids g of one group of 2^l grids at level l. Entry k < 4 lies in k * 4 to (k + 1) * 4 - 1; the other 8 entries are distinct blocks, none of them a pivot block of that list. d_inv[l, g] is the same for all grids g of one group of 2^l grids at level l.
All inputs are finite; a program needn't handle non-finite values.
Results may differ from the reference program's by a relative error of at most 0.0067.
Values may be sent and summed in bfloat16 or wider, within the bound.
A program may use at most 64 MiB of HBM per device.

```python
import jax
import jax.numpy as jnp
from jax import lax

M = 4096
W = 1024
LISTED = 8
GRIDS = 2
LEVELS = 1
FINAL = 2
PIVOTS = 4
BLOCK = 256
NBLOCKS = 16
N_ROW = 4


def order_for(key, height, grid_pos):
    group_seed = jax.random.fold_in(jax.random.fold_in(key, 1000 + height), grid_pos >> height)
    pivot_key, list_key = jax.random.split(group_seed)
    spacing = NBLOCKS // PIVOTS
    offsets = jax.random.randint(pivot_key, (PIVOTS,), 0, spacing, dtype=jnp.int32)
    pivots = jnp.arange(PIVOTS, dtype=jnp.int32) * spacing + offsets
    scores = jax.random.permutation(list_key, NBLOCKS).astype(jnp.int32)
    numbers = jnp.arange(NBLOCKS, dtype=jnp.int32)
    is_pivot = jnp.any(numbers[:, None] == pivots[None, :], axis=1)
    scores = jnp.where(is_pivot, scores + NBLOCKS, scores)
    listed = jnp.argsort(scores, stable=True)[:LISTED].astype(jnp.int32)
    return jnp.concatenate([pivots, listed]).astype(jnp.int32)


def draw_blocks(key, part):
    grid_ids = jnp.arange(GRIDS, dtype=jnp.int32)
    layers = [jax.vmap(lambda grid_pos: order_for(key, height, grid_pos))(grid_ids) for height in range(LEVELS)]
    return jnp.stack(layers).astype(jnp.int32)


def inverse_for(key, height, grid_pos):
    group_seed = jax.random.fold_in(jax.random.fold_in(key, 2000 + height), grid_pos >> height)
    random_part = jnp.clip(jax.random.normal(group_seed, (W, W), jnp.float32), -4.0, 4.0)
    root = jnp.sqrt(jnp.float32(W))
    return (jnp.eye(W, dtype=jnp.float32) + random_part / root) * (0.25 / root)


def draw_d_inv(key, part):
    grid_ids = jnp.arange(GRIDS, dtype=jnp.int32)
    layers = [jax.vmap(lambda grid_pos: inverse_for(key, height, grid_pos))(grid_ids) for height in range(LEVELS)]
    return jnp.stack(layers).astype(jnp.bfloat16)


def shard_levels(own_key, shape, cuts, smallest, largest):
    loudness = 1.0
    for dim, shards_of in cuts:
        draws = jax.random.uniform(jax.random.fold_in(jax.random.fold_in(own_key, 6), dim), (shards_of,), jnp.float32, smallest / len(cuts), largest / len(cuts))
        loudness = loudness * jnp.repeat(jnp.exp(draws), shape[dim] // shards_of).reshape((-1,) + (1,) * (len(shape) - 1 - dim))
    return loudness


def noise(own_key, dims, width, reach, cuts=(), kind=jnp.bfloat16):
    entries = jax.random.normal(own_key, dims, jnp.float32) * width
    if len(cuts) > 0:
        entries = shard_levels(own_key, dims, cuts, -0.22, 0.18) * entries
    return jnp.clip(entries, min=-reach, max=reach).astype(kind)


def setup_inputs(seed: int = 0) -> dict:
    key_of = jax.random.split(jax.random.key(seed), 4)
    return {
        "schur": noise(key_of[0], (GRIDS, M, M), 1.0, 6.0, ((0, 2), (1, 4), (2, 4))),
        "d_inv": draw_d_inv(jax.random.fold_in(key_of[3], 71), 0),
        "blocks": draw_blocks(jax.random.fold_in(key_of[3], 71), 0),
    }


def eliminate(current, chosen, inverse):
    current = current.astype(jnp.float32)
    within = jnp.arange(BLOCK, dtype=jnp.int32)
    pivot_cols = (chosen[:PIVOTS, None] * BLOCK + within[None, :]).reshape(-1).astype(jnp.int32)
    listed_rows = (chosen[PIVOTS:, None] * BLOCK + within[None, :]).reshape(-1).astype(jnp.int32)
    left_panel = current[listed_rows][:, pivot_cols].astype(jnp.bfloat16).astype(jnp.float32)
    upper_panel = current[pivot_cols][:, listed_rows].astype(jnp.bfloat16).astype(jnp.float32)
    scaled = jnp.dot(left_panel, inverse.astype(jnp.float32), preferred_element_type=jnp.float32)
    scaled = scaled.astype(jnp.bfloat16).astype(jnp.float32)
    change = jnp.dot(scaled, upper_panel, preferred_element_type=jnp.float32)
    spread = jnp.zeros((change.shape[0], current.shape[1]), change.dtype).at[:, listed_rows].set(change)
    updated = current.at[listed_rows].add(-spread)
    return updated.astype(jnp.bfloat16)


def reference(schur, d_inv, blocks):
    stored = schur
    for height in range(LEVELS):
        stride = 2 ** height
        chosen_all = blocks[height, ::stride]
        inverse_all = d_inv[height, ::stride]
        result = lax.map(lambda packed: eliminate(packed[0], packed[1], packed[2]), (stored, chosen_all, inverse_all))
        stored = result[0::2].astype(jnp.float32) + result[1::2].astype(jnp.float32)
    final_tiles = stored.astype(jnp.bfloat16)
    quarter = M // N_ROW
    share_rows = quarter // FINAL
    shaped = final_tiles.reshape(GRIDS // FINAL, N_ROW, FINAL, share_rows, M)
    grid_ids = jnp.arange(GRIDS, dtype=jnp.int32)
    reverse = jnp.zeros((GRIDS,), jnp.int32)
    for height in range(LEVELS):
        reverse = reverse + ((grid_ids >> height) & 1) * (2 ** (LEVELS - 1 - height))
    picked = shaped[grid_ids // FINAL, :, reverse]
    return picked.reshape(GRIDS, M // FINAL, M)
```

```python
import functools

import jax
import jax.numpy as jnp
from jax import lax
from jax.experimental import pallas as pl
from jax.experimental.pallas import tpu as pltpu
from jax.sharding import PartitionSpec as P

MESH = pl.DeviceIdType.MESH


def swapped(block, axis, apart):
    count = lax.axis_size(axis)
    route = []
    for low in range(count):
        high = low | 1 << apart
        if high != low and high < count:
            route += [(low, high), (high, low)]
    return lax.ppermute(block, axis, route)


def unchanged(tile_rows, other_rows):
    return tile_rows


def flipped(index, bits):
    bit = 1
    while bit <= bits:
        if bits & bit:
            index = index + bit - 2 * bit * lax.rem(lax.div(index, bit), 2)
        bit *= 2
    return index


class Gather:
    def __init__(self, axis, own, place, sems):
        self.count = lax.axis_size(axis)
        me = lax.axis_index(axis)
        self.copies = {}
        for s in range(1, self.count):
            low = s & -s
            rest = s ^ low
            held = flipped(me, rest)
            self.copies[s] = pltpu.make_async_remote_copy(
                src_ref=own if rest == 0 else place(held),
                dst_ref=place(held),
                send_sem=sems[0].at[s - 1],
                recv_sem=sems[1].at[s - 1],
                device_id={axis: flipped(me, low)},
                device_id_type=MESH,
            )
        self.waited = set()

    def start(self):
        for s in reversed(range(1, self.count)):
            if s & (s - 1) == 0:
                self.copies[s].start()

    def arrive(self, s):
        if s not in self.waited:
            self.waited.add(s)
            self.copies[s].wait_recv()

    def forward(self):
        for rest in reversed(range(2, self.count)):
            lows = [low for low in range(1, rest) if low & (low - 1) == 0 and low < (rest & -rest)]
            if lows:
                self.arrive(rest)
                for low in lows:
                    self.copies[rest | low].start()

    def finish(self):
        for s in range(1, self.count):
            self.arrive(s)

    def sent(self):
        for s in range(1, self.count):
            self.copies[s].wait_send()


def eliminate_kernel(
    chunk,
    tile_ref,
    left_ref,
    upper_ref,
    inv_ref,
    out_ref,
    tile,
    left,
    upper,
    inv,
    product,
    given,
    received,
    local_sems,
    inv_col_sems,
    inv_row_sems,
    upper_sems,
    left_sems,
    swap_sems,
):
    row_pos = lax.axis_index("row")
    col_pos = lax.axis_index("col")
    grid_pos = lax.axis_index("grid")
    n_rows = lax.axis_size("row")
    n_cols = lax.axis_size("col")
    rows = tile.shape[0]
    half = rows // 2
    per_half = half // chunk
    width = inv.shape[0]
    piece = left_ref.shape[1]
    slab = width // n_rows
    bit_value = lax.rem(grid_pos, 2)
    partner = flipped(grid_pos, 1)

    locals_ = [
        pltpu.make_async_copy(
            inv_ref.at[pl.ds(row_pos * slab, slab), :],
            inv.at[pl.ds(row_pos * slab, slab), pl.ds(pl.multiple_of(col_pos * piece, piece), piece)],
            local_sems.at[0],
        ),
        pltpu.make_async_copy(upper_ref, upper.at[pl.ds(row_pos * slab, slab), :], local_sems.at[1]),
        pltpu.make_async_copy(
            left_ref, left.at[:, pl.ds(pl.multiple_of(col_pos * piece, piece), piece)], local_sems.at[2]
        ),
        pltpu.make_async_copy(tile_ref, tile, local_sems.at[3]),
    ]
    for copy in locals_:
        copy.start()

    barrier = pltpu.get_barrier_semaphore()
    peers = [{"grid": partner}]
    for axis, count in (("row", n_rows), ("col", n_cols)):
        bit = 1
        while bit < count:
            peers.append({axis: flipped(lax.axis_index(axis), bit)})
            bit *= 2
    for peer in peers:
        pl.semaphore_signal(barrier, inc=1, device_id=peer, device_id_type=MESH)
    pl.semaphore_wait(barrier, len(peers))

    def inv_place(held):
        return inv.at[
            pl.ds(row_pos * slab, slab), pl.ds(pl.multiple_of(held * piece, piece), piece)
        ]

    def slab_place(held):
        return inv.at[pl.ds(held * slab, slab), :]

    def upper_place(held):
        return upper.at[pl.ds(held * slab, slab), :]

    starts = [(1 - bit_value) * half + i * chunk for i in range(per_half)]
    starts += [bit_value * half + i * chunk for i in range(per_half)]

    def left_gather(i):
        def place(held):
            return left.at[
                pl.ds(starts[i], chunk), pl.ds(pl.multiple_of(held * piece, piece), piece)
            ]

        return Gather(
            "col",
            left_ref.at[pl.ds(starts[i], chunk), :],
            place,
            (left_sems.at[0, i], left_sems.at[1, i]),
        )

    inv_col = Gather(
        "col",
        inv_ref.at[pl.ds(row_pos * slab, slab), :],
        inv_place,
        (inv_col_sems.at[0], inv_col_sems.at[1]),
    )
    inv_row = Gather(
        "row", slab_place(row_pos), slab_place, (inv_row_sems.at[0], inv_row_sems.at[1])
    )
    upper_all = Gather(
        "row", upper_ref, upper_place, (upper_sems.at[0], upper_sems.at[1])
    )
    lefts = [left_gather(i) for i in range(2 * per_half)]

    inv_col.start()
    upper_all.start()
    lefts[0].start()
    inv_col.forward()
    lefts[1].start()
    inv_col.finish()
    locals_[0].wait()
    inv_row.start()
    upper_all.forward()
    lefts[0].forward()
    lefts[2].start()
    inv_row.forward()
    lefts[1].forward()
    lefts[3].start()
    upper_all.finish()
    inv_row.finish()
    locals_[1].wait()

    @pl.loop(0, width // chunk)
    def _(i):
        at = pl.ds(pl.multiple_of(i * chunk, chunk), chunk)
        product[at, :] = jnp.dot(
            inv[at, :], upper[...], preferred_element_type=jnp.float32
        ).astype(jnp.bfloat16)

    locals_[2].wait()
    locals_[3].wait()

    def eliminated(i):
        at = pl.ds(pl.multiple_of(starts[i], chunk), chunk)
        change = jnp.dot(left[at, :], product[...], preferred_element_type=jnp.float32)
        return (tile[at, :].astype(jnp.float32) - change).astype(jnp.bfloat16)

    swaps = []
    for i in range(2 * per_half):
        ahead = i + 2
        if ahead < 2 * per_half:
            lefts[ahead].forward()
        if ahead + 2 < 2 * per_half:
            lefts[ahead + 2].start()
        lefts[i].finish()
        if i < per_half:
            at = pl.ds(i * chunk, chunk)
            given[at, :] = eliminated(i)
            swap = pltpu.make_async_remote_copy(
                src_ref=given.at[at, :],
                dst_ref=received.at[at, :],
                send_sem=swap_sems.at[0, i],
                recv_sem=swap_sems.at[1, i],
                device_id={"grid": partner},
                device_id_type=MESH,
            )
            swap.start()
            swaps.append(swap)
        else:
            at = pl.ds((i - per_half) * chunk, chunk)
            kept = eliminated(i).astype(jnp.float32)
            swaps[i - per_half].wait_recv()
            out_ref[at, :] = (kept + received[at, :].astype(jnp.float32)).astype(out_ref.dtype)
    for gather in [inv_col, inv_row, upper_all] + lefts:
        gather.sent()
    for swap in swaps:
        swap.wait_send()


def first_level(tile, inverse, chosen, out_dtype):
    n_rows = lax.axis_size("row")
    n_cols = lax.axis_size("col")
    rows, cols = tile.shape
    width = inverse.shape[0]
    block = width // n_rows
    row_start = lax.axis_index("row") * rows
    col_pos = lax.axis_index("col")
    col_start = col_pos * cols
    pivots = chosen[:n_rows]
    listed = chosen[n_rows:]
    row_ids = (row_start + jnp.arange(rows, dtype=jnp.int32)) // block
    col_ids = (col_start + jnp.arange(cols, dtype=jnp.int32)) // block
    row_keep = jnp.any(row_ids[:, None] == listed[None, :], axis=1)
    col_keep = jnp.any(col_ids[:, None] == listed[None, :], axis=1)
    zero = jnp.zeros((), tile.dtype)
    left = lax.dynamic_slice_in_dim(tile, pivots[col_pos] * block - col_start, block, 1)
    left = jnp.where(row_keep[:, None], left, zero)
    upper = lax.dynamic_slice_in_dim(
        tile, pivots[lax.axis_index("row")] * block - row_start, block, 0
    )
    upper = jnp.where(col_keep[None, :], upper, zero)
    chunk = rows // 4
    bf16 = jnp.bfloat16
    dma = pltpu.SemaphoreType.DMA
    return pl.pallas_call(
        functools.partial(eliminate_kernel, chunk),
        out_shape=jax.ShapeDtypeStruct((rows // 2, cols), out_dtype),
        in_specs=[pl.BlockSpec(memory_space=pl.ANY)] * 4,
        out_specs=pl.BlockSpec(memory_space=pltpu.VMEM),
        scratch_shapes=[
            pltpu.VMEM((rows, cols), bf16),
            pltpu.VMEM((rows, width), bf16),
            pltpu.VMEM((width, cols), bf16),
            pltpu.VMEM((width, width), bf16),
            pltpu.VMEM((width, cols), bf16),
            pltpu.VMEM((rows // 2, cols), bf16),
            pltpu.VMEM((rows // 2, cols), bf16),
            dma((4,)),
            dma((2, n_cols - 1)),
            dma((2, n_rows - 1)),
            dma((2, n_rows - 1)),
            dma((2, 4, n_cols - 1)),
            dma((2, 2)),
        ],
        compiler_params=pltpu.CompilerParams(
            collective_id=0, has_side_effects=True, vmem_limit_bytes=40 * 1024 * 1024
        ),
    )(tile, left, upper, inverse)


def shards(schur, d_inv, blocks):
    n_rows = lax.axis_size("row")
    grid_pos = lax.axis_index("grid")
    row_pos = lax.axis_index("row")
    col_pos = lax.axis_index("col")
    levels = blocks.shape[0]
    quarter_rows = schur.shape[1]
    local_cols = schur.shape[2]
    width = d_inv.shape[2]
    block = width // n_rows
    col_start = col_pos * local_cols
    col_ids = (col_start + jnp.arange(local_cols, dtype=jnp.int32)) // block
    current = first_level(
        schur[0], d_inv[0, 0], blocks[0, 0], jnp.bfloat16 if levels == 1 else jnp.float32
    )
    row_shift = (grid_pos & 1) * (quarter_rows // 2)
    for height in range(1, levels):
        rows_here = current.shape[0]
        count = rows_here // block
        chosen = blocks[height, 0]
        pivots = chosen[:n_rows]
        listed = chosen[n_rows:]
        row_start = row_pos * quarter_rows + row_shift
        col_keep = jnp.any(col_ids[:, None] == listed[None, :], axis=1)
        left_piece = lax.dynamic_slice_in_dim(
            current, pivots[col_pos] * block - col_start, block, 1
        ).astype(jnp.bfloat16)
        left_panel = lax.all_gather(left_piece, "col", axis=1, tiled=True)
        part = min(block, rows_here)
        offset = pivots[row_pos] * block - row_start
        upper_piece = jnp.zeros((block, local_cols), jnp.bfloat16)
        for start in range(0, block, part):
            inside = offset + start
            owned = (inside >= 0) & (inside < rows_here)
            rows_of = lax.dynamic_slice_in_dim(
                current, jnp.clip(inside, 0, rows_here - part), part, 0
            )
            upper_piece = lax.dynamic_update_slice_in_dim(
                upper_piece, jnp.where(owned, rows_of, 0.0).astype(jnp.bfloat16), start, 0
            )
        for member_bit in range(height):
            upper_piece = upper_piece + swapped(upper_piece, "grid", member_bit)
        upper_panel = lax.all_gather(upper_piece, "row", axis=0, tiled=True)
        upper_panel = jnp.where(col_keep[None, :], upper_panel, jnp.zeros((), jnp.bfloat16))
        inverse_full = lax.all_gather(d_inv[height, 0], "col", axis=1, tiled=True)

        def update_block(tile_rows, left_rows):
            scaled = jnp.dot(left_rows, inverse_full, preferred_element_type=jnp.float32).astype(
                jnp.bfloat16
            )
            return tile_rows - jnp.dot(scaled, upper_panel, preferred_element_type=jnp.float32)

        pieces = []
        for start in range(0, rows_here, part):
            row_id = (row_start + start) // block
            pieces.append(
                lax.cond(
                    jnp.any(row_id == listed),
                    update_block,
                    unchanged,
                    current[start : start + part],
                    left_panel[start : start + part],
                )
            )
        updated = jnp.concatenate(pieces, axis=0).astype(jnp.bfloat16)
        bit_value = grid_pos >> height & 1
        half_rows = rows_here // 2
        kept = lax.dynamic_slice_in_dim(updated, bit_value * half_rows, half_rows, 0)
        given = lax.dynamic_slice_in_dim(updated, (1 - bit_value) * half_rows, half_rows, 0)
        received = swapped(given, "grid", height)
        current = kept.astype(jnp.float32) + received.astype(jnp.float32)
        row_shift = row_shift + bit_value * half_rows
    return current.astype(jnp.bfloat16)[None]


def solution(mesh):
    return jax.shard_map(
        shards,
        mesh=mesh,
        in_specs=(P("grid", "row", "col"), P(None, "grid", None, "col"), P(None, "grid", None)),
        out_specs=P("grid", "row", "col"),
        check_vma=False,
    )
```

```python
import functools

import jax
import jax.numpy as jnp
from jax import lax
from jax.experimental import pallas as pl
from jax.experimental.pallas import tpu as pltpu
from jax.sharding import PartitionSpec as P

MESH = pl.DeviceIdType.MESH


def swapped(block, axis, apart):
    count = lax.axis_size(axis)
    route = []
    for low in range(count):
        high = low | 1 << apart
        if high != low and high < count:
            route += [(low, high), (high, low)]
    return lax.ppermute(block, axis, route)


def unchanged(tile_rows, other_rows):
    return tile_rows


def flipped(index, bits):
    bit = 1
    while bit <= bits:
        if bits & bit:
            index = index + bit - 2 * bit * lax.rem(lax.div(index, bit), 2)
        bit *= 2
    return index


class Gather:
    def __init__(self, axis, own, place, sems):
        self.count = lax.axis_size(axis)
        me = lax.axis_index(axis)
        self.copies = {}
        for s in range(1, self.count):
            low = s & -s
            rest = s ^ low
            held = flipped(me, rest)
            self.copies[s] = pltpu.make_async_remote_copy(
                src_ref=own if rest == 0 else place(held),
                dst_ref=place(held),
                send_sem=sems[0].at[s - 1],
                recv_sem=sems[1].at[s - 1],
                device_id={axis: flipped(me, low)},
                device_id_type=MESH,
            )
        self.waited = set()

    def start(self):
        for s in reversed(range(1, self.count)):
            if s & (s - 1) == 0:
                self.copies[s].start()

    def arrive(self, s):
        if s not in self.waited:
            self.waited.add(s)
            self.copies[s].wait_recv()

    def forward(self):
        for rest in reversed(range(2, self.count)):
            lows = [low for low in range(1, rest) if low & (low - 1) == 0 and low < (rest & -rest)]
            if lows:
                self.arrive(rest)
                for low in lows:
                    self.copies[rest | low].start()

    def finish(self):
        for s in range(1, self.count):
            self.arrive(s)

    def sent(self):
        for s in range(1, self.count):
            self.copies[s].wait_send()


class Relay:
    def __init__(self, axis, own, place, sems):
        self.count = lax.axis_size(axis)
        self.me = lax.axis_index(axis)
        self.copies = {}
        for side, step in enumerate((1, -1)):
            for d in range(self.count - 1):
                held = jnp.clip(self.me - step * d, 0, self.count - 1)
                self.copies[side, d] = pltpu.make_async_remote_copy(
                    src_ref=own if d == 0 else place(held),
                    dst_ref=place(held),
                    send_sem=sems[0].at[side, d],
                    recv_sem=sems[1].at[side, d],
                    device_id={axis: jnp.clip(self.me + step, 0, self.count - 1)},
                    device_id_type=MESH,
                )

    def sends(self, side, d):
        if side == 0:
            return (self.me >= d) & (self.me + 1 < self.count)
        return (self.me + d < self.count) & (self.me >= 1)

    def receives(self, side, d):
        if side == 0:
            return self.me >= d + 1
        return self.me + d + 1 < self.count

    def start(self):
        for side in range(2):
            pl.when(self.sends(side, 0))(self.copies[side, 0].start)

    def hop(self, d):
        for side in range(2):
            pl.when(self.receives(side, d))(self.copies[side, d].wait_recv)
            if d + 1 < self.count - 1:
                pl.when(self.sends(side, d + 1))(self.copies[side, d + 1].start)

    def forward(self):
        for d in range(self.count - 2):
            self.hop(d)

    def finish(self):
        self.hop(self.count - 2)

    def sent(self):
        for side in range(2):
            for d in range(self.count - 1):
                pl.when(self.sends(side, d))(self.copies[side, d].wait_send)


def eliminate_kernel(
    block,
    parts,
    flags,
    tile_ref,
    left_ref,
    upper_ref,
    inv_ref,
    out_ref,
    tile,
    left,
    upper,
    inv,
    product,
    change,
    given,
    received,
    local_sems,
    inv_col_sems,
    inv_row_sems,
    upper_sems,
    left_sems,
    swap_sems,
):
    row_pos = lax.axis_index("row")
    col_pos = lax.axis_index("col")
    grid_pos = lax.axis_index("grid")
    n_rows = lax.axis_size("row")
    n_cols = lax.axis_size("col")
    row_blocks = tile.shape[0] // block
    width = inv.shape[0]
    piece = inv_ref.shape[1]
    slab = width // n_rows
    chunk = block // parts
    half = row_blocks // 2
    bit_value = lax.rem(grid_pos, 2)
    partner = flipped(grid_pos, 1)

    inv_copy = pltpu.make_async_copy(
        inv_ref.at[pl.ds(row_pos * slab, slab), :],
        inv.at[pl.ds(row_pos * slab, slab), pl.ds(pl.multiple_of(col_pos * piece, piece), piece)],
        local_sems.at[0],
    )
    tile_copy = pltpu.make_async_copy(tile_ref, tile, local_sems.at[1])
    upper_copy = pltpu.make_async_copy(
        upper_ref, upper.at[pl.ds(row_pos * slab, slab), :], local_sems.at[2]
    )
    left_copy = pltpu.make_async_copy(
        left_ref,
        left.at[:, pl.ds(pl.multiple_of(col_pos * piece, piece), piece)],
        local_sems.at[3],
    )
    for copy in (inv_copy, upper_copy, left_copy, tile_copy):
        copy.start()

    barrier = pltpu.get_barrier_semaphore()
    bit = 1
    while bit < n_rows:
        peer = {"row": flipped(row_pos, bit)}
        pl.semaphore_signal(barrier, inc=1, device_id=peer, device_id_type=MESH)
        bit *= 2
    pl.semaphore_signal(barrier, inc=1, device_id={"grid": partner}, device_id_type=MESH)
    for near, there in ((col_pos - 1, col_pos >= 1), (col_pos + 1, col_pos + 1 < n_cols)):

        @pl.when(there)
        def _():
            pl.semaphore_signal(
                barrier,
                inc=1,
                device_id={"col": jnp.clip(near, 0, n_cols - 1)},
                device_id_type=MESH,
            )

    fixed = n_rows.bit_length()
    middle = (col_pos >= 1) & (col_pos + 1 < n_cols)

    @pl.when(middle)
    def _():
        pl.semaphore_wait(barrier, fixed + 2)

    @pl.when(jnp.logical_not(middle))
    def _():
        pl.semaphore_wait(barrier, fixed + 1)

    def inv_place(held):
        return inv.at[
            pl.ds(row_pos * slab, slab), pl.ds(pl.multiple_of(held * piece, piece), piece)
        ]

    def slab_place(held):
        return inv.at[pl.ds(held * slab, slab), :]

    def upper_place(held):
        return upper.at[pl.ds(held * slab, slab), :]

    inv_col = Relay(
        "col",
        inv_ref.at[pl.ds(row_pos * slab, slab), :],
        inv_place,
        (inv_col_sems.at[0], inv_col_sems.at[1]),
    )
    inv_row = Gather(
        "row", slab_place(row_pos), slab_place, (inv_row_sems.at[0], inv_row_sems.at[1])
    )
    upper_all = Gather(
        "row", upper_ref, upper_place, (upper_sems.at[0], upper_sems.at[1])
    )

    def left_gather(unit):
        def place(held):
            return left.at[
                pl.ds(unit * chunk, chunk), pl.ds(pl.multiple_of(held * piece, piece), piece)
            ]

        return Relay(
            "col",
            left_ref.at[pl.ds(unit * chunk, chunk), :],
            place,
            (left_sems.at[0, unit], left_sems.at[1, unit]),
        )

    lefts = [left_gather(unit) for unit in range((row_blocks - 1) * parts)]

    given_start = (1 - bit_value) * half

    inv_col.start()
    upper_all.start()
    units = len(lefts)
    ahead = 2
    for unit in range(min(ahead, units)):
        lefts[unit].start()
    begun = min(ahead, units)
    inv_col.forward()
    inv_col.finish()
    inv_copy.wait()
    inv_row.start()
    passed = 0

    def pump(upto):
        nonlocal passed, begun
        while passed < min(upto, units):
            if begun < units:
                lefts[begun].start()
                begun += 1
            lefts[passed].forward()
            passed += 1

    pump(1)
    upper_all.forward()
    pump(2)
    inv_row.forward()
    pump(3)
    upper_all.finish()
    inv_row.finish()
    upper_copy.wait()

    @pl.loop(0, width // block)
    def _(i):
        at = pl.ds(pl.multiple_of(i * block, block), block)
        product[at, :] = jnp.dot(
            inv[at, :], upper[...], preferred_element_type=jnp.float32
        ).astype(jnp.bfloat16)

    def eliminated(place, part):
        row_block = lax.rem(given_start + place, row_blocks)
        at = pl.ds(pl.multiple_of(row_block * block + part * chunk, chunk), chunk)
        total = tile[at, :].astype(jnp.float32)
        if place < row_blocks - 1:
            total = total - flags[place : place + 1, :] * change[
                pl.ds(place * block + part * chunk, chunk), :
            ]
        if place > 0:
            total = total - flags[row_blocks + place : row_blocks + place + 1, :] * change[
                pl.ds((place - 1) * block + part * chunk, chunk), :
            ]
        return total.astype(jnp.bfloat16)

    left_copy.wait()
    tile_copy.wait()
    swaps = []
    for place in range(row_blocks):
        for part in range(parts):
            if place < row_blocks - 1:
                unit = place * parts + part
                pump(unit + 1 + 1)
                lefts[unit].finish()
                at = pl.ds(unit * chunk, chunk)
                change[at, :] = jnp.dot(
                    left[at, :], product[...], preferred_element_type=jnp.float32
                )
            if place < half:
                at = pl.ds(place * block + part * chunk, chunk)
                given[at, :] = eliminated(place, part)
                swap = pltpu.make_async_remote_copy(
                    src_ref=given.at[at, :],
                    dst_ref=received.at[at, :],
                    send_sem=swap_sems.at[0, len(swaps)],
                    recv_sem=swap_sems.at[1, len(swaps)],
                    device_id={"grid": partner},
                    device_id_type=MESH,
                )
                swap.start()
                swaps.append(swap)
            else:
                at = pl.ds((place - half) * block + part * chunk, chunk)
                kept = eliminated(place, part).astype(jnp.float32)
                swaps[(place - half) * parts + part].wait_recv()
                out_ref[at, :] = (kept + received[at, :].astype(jnp.float32)).astype(out_ref.dtype)
    for gather in [inv_col, inv_row, upper_all] + lefts:
        gather.sent()
    for swap in swaps:
        swap.wait_send()


def cut_kernel(block, chosen, left_ref, upper_ref, left_out, upper_out, flags_out):
    row_pos = lax.axis_index("row")
    col_pos = lax.axis_index("col")
    n_rows = lax.axis_size("row")
    row_blocks = left_ref.shape[0] // block
    col_blocks = upper_ref.shape[1] // block

    def is_listed(number):
        found = jnp.int32(0)
        for k in range(n_rows, chosen.shape[0]):
            found = found + (chosen[k] == number).astype(jnp.int32)
        return found.astype(jnp.float32)

    given_start = (1 - lax.rem(lax.axis_index("grid"), 2)) * (row_blocks // 2)
    own_row = lax.rem(chosen[row_pos], row_blocks)
    pivot_place = lax.rem(own_row + row_blocks - given_start, row_blocks)
    for slot in range(row_blocks - 1):
        place = slot + (slot >= pivot_place).astype(jnp.int32)
        row_block = lax.rem(given_start + place, row_blocks)
        values = left_ref[pl.ds(pl.multiple_of(row_block * block, block), block), :]
        kept = values.astype(jnp.float32) * is_listed(row_pos * row_blocks + row_block)
        left_out[pl.ds(slot * block, block), :] = kept.astype(left_out.dtype)
    for c in range(col_blocks):
        span = pl.ds(c * block, block)
        kept = upper_ref[:, span].astype(jnp.float32) * is_listed(col_pos * col_blocks + c)
        upper_out[:, span] = kept.astype(upper_out.dtype)
    for place in range(row_blocks):
        for row, holds in ((place, pivot_place > place), (row_blocks + place, pivot_place < place)):
            flags_out[row : row + 1, :] = jnp.full(
                (1, flags_out.shape[1]), holds.astype(jnp.int32).astype(jnp.float32)
            )


def first_level(tile, inverse, chosen, out_dtype):
    n_rows = lax.axis_size("row")
    n_cols = lax.axis_size("col")
    rows, cols = tile.shape
    width = inverse.shape[0]
    block = width // n_rows
    slots = rows // block - 1
    parts = 2
    bf16 = jnp.bfloat16
    dma = pltpu.SemaphoreType.DMA
    left, upper, flags = pl.pallas_call(
        functools.partial(cut_kernel, block),
        grid_spec=pltpu.PrefetchScalarGridSpec(
            num_scalar_prefetch=1,
            grid=(1,),
            in_specs=[
                pl.BlockSpec(
                    (rows, block),
                    lambda i, chosen: (0, lax.rem(chosen[lax.axis_index("col")], cols // block)),
                ),
                pl.BlockSpec(
                    (block, cols),
                    lambda i, chosen: (lax.rem(chosen[lax.axis_index("row")], rows // block), 0),
                ),
            ],
            out_specs=[
                pl.BlockSpec((slots * block, block), lambda i, chosen: (0, 0)),
                pl.BlockSpec((block, cols), lambda i, chosen: (0, 0)),
                pl.BlockSpec((2 * (slots + 1), cols), lambda i, chosen: (0, 0)),
            ],
        ),
        out_shape=[
            jax.ShapeDtypeStruct((slots * block, block), bf16),
            jax.ShapeDtypeStruct((block, cols), bf16),
            jax.ShapeDtypeStruct((2 * (slots + 1), cols), jnp.float32),
        ],
    )(chosen, tile, tile)
    return pl.pallas_call(
        functools.partial(eliminate_kernel, block, parts),
        out_shape=jax.ShapeDtypeStruct((rows // 2, cols), out_dtype),
        in_specs=[pl.BlockSpec(memory_space=pltpu.VMEM)] + [pl.BlockSpec(memory_space=pl.ANY)] * 4,
        out_specs=pl.BlockSpec(memory_space=pltpu.VMEM),
        scratch_shapes=[
            pltpu.VMEM((rows, cols), bf16),
            pltpu.VMEM((slots * block, width), bf16),
            pltpu.VMEM((width, cols), bf16),
            pltpu.VMEM((width, width), bf16),
            pltpu.VMEM((width, cols), bf16),
            pltpu.VMEM((slots * block, cols), jnp.float32),
            pltpu.VMEM((rows // 2, cols), bf16),
            pltpu.VMEM((rows // 2, cols), bf16),
            dma((4,)),
            dma((2, 2, n_cols - 1)),
            dma((2, n_rows - 1)),
            dma((2, n_rows - 1)),
            dma((2, slots * parts, 2, n_cols - 1)),
            dma((2, (slots + 1) // 2 * parts)),
        ],
        compiler_params=pltpu.CompilerParams(
            collective_id=0, has_side_effects=True, vmem_limit_bytes=56 * 1024 * 1024
        ),
    )(flags, tile, left, upper, inverse)


def shards(schur, d_inv, blocks):
    n_rows = lax.axis_size("row")
    grid_pos = lax.axis_index("grid")
    row_pos = lax.axis_index("row")
    col_pos = lax.axis_index("col")
    levels = blocks.shape[0]
    quarter_rows = schur.shape[1]
    local_cols = schur.shape[2]
    width = d_inv.shape[2]
    block = width // n_rows
    col_start = col_pos * local_cols
    col_ids = (col_start + jnp.arange(local_cols, dtype=jnp.int32)) // block
    current = first_level(
        schur[0], d_inv[0, 0], blocks[0, 0], jnp.bfloat16 if levels == 1 else jnp.float32
    )
    row_shift = (grid_pos & 1) * (quarter_rows // 2)
    for height in range(1, levels):
        rows_here = current.shape[0]
        count = rows_here // block
        chosen = blocks[height, 0]
        pivots = chosen[:n_rows]
        listed = chosen[n_rows:]
        row_start = row_pos * quarter_rows + row_shift
        col_keep = jnp.any(col_ids[:, None] == listed[None, :], axis=1)
        left_piece = lax.dynamic_slice_in_dim(
            current, pivots[col_pos] * block - col_start, block, 1
        ).astype(jnp.bfloat16)
        left_panel = lax.all_gather(left_piece, "col", axis=1, tiled=True)
        part = min(block, rows_here)
        offset = pivots[row_pos] * block - row_start
        upper_piece = jnp.zeros((block, local_cols), jnp.bfloat16)
        for start in range(0, block, part):
            inside = offset + start
            owned = (inside >= 0) & (inside < rows_here)
            rows_of = lax.dynamic_slice_in_dim(
                current, jnp.clip(inside, 0, rows_here - part), part, 0
            )
            upper_piece = lax.dynamic_update_slice_in_dim(
                upper_piece, jnp.where(owned, rows_of, 0.0).astype(jnp.bfloat16), start, 0
            )
        for member_bit in range(height):
            upper_piece = upper_piece + swapped(upper_piece, "grid", member_bit)
        upper_panel = lax.all_gather(upper_piece, "row", axis=0, tiled=True)
        upper_panel = jnp.where(col_keep[None, :], upper_panel, jnp.zeros((), jnp.bfloat16))
        inverse_full = lax.all_gather(d_inv[height, 0], "col", axis=1, tiled=True)

        def update_block(tile_rows, left_rows):
            scaled = jnp.dot(left_rows, inverse_full, preferred_element_type=jnp.float32).astype(
                jnp.bfloat16
            )
            return tile_rows - jnp.dot(scaled, upper_panel, preferred_element_type=jnp.float32)

        pieces = []
        for start in range(0, rows_here, part):
            row_id = (row_start + start) // block
            pieces.append(
                lax.cond(
                    jnp.any(row_id == listed),
                    update_block,
                    unchanged,
                    current[start : start + part],
                    left_panel[start : start + part],
                )
            )
        updated = jnp.concatenate(pieces, axis=0).astype(jnp.bfloat16)
        bit_value = grid_pos >> height & 1
        half_rows = rows_here // 2
        kept = lax.dynamic_slice_in_dim(updated, bit_value * half_rows, half_rows, 0)
        given = lax.dynamic_slice_in_dim(updated, (1 - bit_value) * half_rows, half_rows, 0)
        received = swapped(given, "grid", height)
        current = kept.astype(jnp.float32) + received.astype(jnp.float32)
        row_shift = row_shift + bit_value * half_rows
    return current.astype(jnp.bfloat16)[None]


def solution(mesh):
    return jax.shard_map(
        shards,
        mesh=mesh,
        in_specs=(P("grid", "row", "col"), P(None, "grid", None, "col"), P(None, "grid", None)),
        out_specs=P("grid", "row", "col"),
        check_vma=False,
    )
```

```python
import functools

import jax
import jax.numpy as jnp
from jax import lax
from jax.experimental import pallas as pl
from jax.experimental.pallas import tpu as pltpu
from jax.sharding import PartitionSpec as P

MESH = pl.DeviceIdType.MESH


def swapped(block, axis, apart):
    count = lax.axis_size(axis)
    route = []
    for low in range(count):
        high = low | 1 << apart
        if high != low and high < count:
            route += [(low, high), (high, low)]
    return lax.ppermute(block, axis, route)


def unchanged(tile_rows, other_rows):
    return tile_rows


def flipped(index, bits):
    bit = 1
    while bit <= bits:
        if bits & bit:
            index = index + bit - 2 * bit * lax.rem(lax.div(index, bit), 2)
        bit *= 2
    return index


class Gather:
    def __init__(self, axis, own, place, sems):
        self.count = lax.axis_size(axis)
        me = lax.axis_index(axis)
        self.copies = {}
        for s in range(1, self.count):
            low = s & -s
            rest = s ^ low
            held = flipped(me, rest)
            self.copies[s] = pltpu.make_async_remote_copy(
                src_ref=own if rest == 0 else place(held),
                dst_ref=place(held),
                send_sem=sems[0].at[s - 1],
                recv_sem=sems[1].at[s - 1],
                device_id={axis: flipped(me, low)},
                device_id_type=MESH,
            )
        self.waited = set()

    def start(self):
        for s in reversed(range(1, self.count)):
            if s & (s - 1) == 0:
                self.copies[s].start()

    def arrive(self, s):
        if s not in self.waited:
            self.waited.add(s)
            self.copies[s].wait_recv()

    def forward(self):
        for rest in reversed(range(2, self.count)):
            lows = [low for low in range(1, rest) if low & (low - 1) == 0 and low < (rest & -rest)]
            if lows:
                self.arrive(rest)
                for low in lows:
                    self.copies[rest | low].start()

    def finish(self):
        for s in range(1, self.count):
            self.arrive(s)

    def sent(self):
        for s in range(1, self.count):
            self.copies[s].wait_send()


class Relay:
    def __init__(self, axis, own, place, sems):
        self.count = lax.axis_size(axis)
        self.me = lax.axis_index(axis)
        self.copies = {}
        for side, step in enumerate((1, -1)):
            for d in range(self.count - 1):
                held = jnp.clip(self.me - step * d, 0, self.count - 1)
                self.copies[side, d] = pltpu.make_async_remote_copy(
                    src_ref=own if d == 0 else place(held),
                    dst_ref=place(held),
                    send_sem=sems[0].at[side, d],
                    recv_sem=sems[1].at[side, d],
                    device_id={axis: jnp.clip(self.me + step, 0, self.count - 1)},
                    device_id_type=MESH,
                )

    def sends(self, side, d):
        if side == 0:
            return (self.me >= d) & (self.me + 1 < self.count)
        return (self.me + d < self.count) & (self.me >= 1)

    def receives(self, side, d):
        if side == 0:
            return self.me >= d + 1
        return self.me + d + 1 < self.count

    def start(self):
        for side in range(2):
            pl.when(self.sends(side, 0))(self.copies[side, 0].start)

    def hop(self, d):
        for side in range(2):
            pl.when(self.receives(side, d))(self.copies[side, d].wait_recv)
            if d + 1 < self.count - 1:
                pl.when(self.sends(side, d + 1))(self.copies[side, d + 1].start)

    def forward(self):
        for d in range(self.count - 2):
            self.hop(d)

    def finish(self):
        self.hop(self.count - 2)

    def sent(self):
        for side in range(2):
            for d in range(self.count - 1):
                pl.when(self.sends(side, d))(self.copies[side, d].wait_send)


def eliminate_kernel(
    block,
    parts,
    flags,
    tile_ref,
    left_ref,
    upper_ref,
    raw_ref,
    inv_ref,
    out_ref,
    tile,
    left,
    upper,
    inv,
    product,
    change,
    given,
    received,
    raw,
    other_flags,
    local_sems,
    inv_col_sems,
    product_all_sems,
    upper_sems,
    left_sems,
    swap_sems,
    early_sems,
):
    row_pos = lax.axis_index("row")
    col_pos = lax.axis_index("col")
    grid_pos = lax.axis_index("grid")
    n_rows = lax.axis_size("row")
    n_cols = lax.axis_size("col")
    row_blocks = tile.shape[0] // block
    col_blocks = tile.shape[1] // block
    width = inv.shape[1]
    piece = inv_ref.shape[1]
    slab = width // n_rows
    chunk = block // parts
    half = row_blocks // 2
    bit_value = lax.rem(grid_pos, 2)
    partner = flipped(grid_pos, 1)

    inv_copy = pltpu.make_async_copy(
        inv_ref.at[pl.ds(row_pos * slab, slab), :],
        inv.at[:, pl.ds(pl.multiple_of(col_pos * piece, piece), piece)],
        local_sems.at[0],
    )
    tile_copy = pltpu.make_async_copy(tile_ref, tile, local_sems.at[1])
    upper_copy = pltpu.make_async_copy(
        upper_ref, upper.at[pl.ds(row_pos * slab, slab), :], local_sems.at[2]
    )
    left_copy = pltpu.make_async_copy(
        left_ref,
        left.at[:, pl.ds(pl.multiple_of(col_pos * piece, piece), piece)],
        local_sems.at[3],
    )
    for copy in (inv_copy, upper_copy, left_copy, tile_copy):
        copy.start()

    barrier = pltpu.get_barrier_semaphore()
    bit = 1
    while bit < n_rows:
        peer = {"row": flipped(row_pos, bit)}
        pl.semaphore_signal(barrier, inc=1, device_id=peer, device_id_type=MESH)
        bit *= 2
    pl.semaphore_signal(barrier, inc=1, device_id={"grid": partner}, device_id_type=MESH)
    for near, there in ((col_pos - 1, col_pos >= 1), (col_pos + 1, col_pos + 1 < n_cols)):

        @pl.when(there)
        def _():
            pl.semaphore_signal(
                barrier,
                inc=1,
                device_id={"col": jnp.clip(near, 0, n_cols - 1)},
                device_id_type=MESH,
            )

    fixed = n_rows.bit_length()
    middle = (col_pos >= 1) & (col_pos + 1 < n_cols)

    @pl.when(middle)
    def _():
        pl.semaphore_wait(barrier, fixed + 2)

    @pl.when(jnp.logical_not(middle))
    def _():
        pl.semaphore_wait(barrier, fixed + 1)

    def inv_place(held):
        return inv.at[:, pl.ds(pl.multiple_of(held * piece, piece), piece)]

    def slab_place(held):
        return product.at[pl.ds(held * slab, slab), :]

    def upper_place(held):
        return upper.at[pl.ds(held * slab, slab), :]

    inv_col = Relay(
        "col",
        inv_ref.at[pl.ds(row_pos * slab, slab), :],
        inv_place,
        (inv_col_sems.at[0], inv_col_sems.at[1]),
    )
    product_all = Gather(
        "row", slab_place(row_pos), slab_place, (product_all_sems.at[0], product_all_sems.at[1])
    )
    upper_all = Gather(
        "row", upper_ref, upper_place, (upper_sems.at[0], upper_sems.at[1])
    )

    def left_gather(unit):
        def place(held):
            return left.at[
                pl.ds(unit * chunk, chunk), pl.ds(pl.multiple_of(held * piece, piece), piece)
            ]

        return Relay(
            "col",
            left_ref.at[pl.ds(unit * chunk, chunk), :],
            place,
            (left_sems.at[0, unit], left_sems.at[1, unit]),
        )

    lefts = [left_gather(unit) for unit in range((row_blocks - 1) * parts)]

    given_start = (1 - bit_value) * half

    inv_col.start()
    upper_all.start()
    early = [
        pltpu.make_async_remote_copy(
            src_ref=source,
            dst_ref=target,
            send_sem=early_sems.at[0, i],
            recv_sem=early_sems.at[1, i],
            device_id={"grid": partner},
            device_id_type=MESH,
        )
        for i, (source, target) in enumerate(
            ((raw_ref, raw), (flags.at[pl.ds(16, 16), :], other_flags))
        )
    ]
    for copy in early:
        copy.start()
    units = len(lefts)
    ahead = 2
    for unit in range(min(ahead, units)):
        lefts[unit].start()
    begun = min(ahead, units)
    inv_col.forward()
    passed = 0

    def pump(upto):
        nonlocal passed, begun
        while passed < min(upto, units):
            if begun < units:
                lefts[begun].start()
                begun += 1
            lefts[passed].forward()
            passed += 1

    upper_all.forward()
    inv_col.finish()
    inv_copy.wait()
    pump(1)
    upper_all.finish()
    upper_copy.wait()
    product[pl.ds(row_pos * slab, slab), :] = jnp.dot(
        inv[...], upper[...], preferred_element_type=jnp.float32
    ).astype(jnp.bfloat16)
    product_all.start()
    pump(2)
    product_all.forward()
    pump(3)
    product_all.finish()

    def pick(flag_ref, start, q):
        return flag_ref[start + q : start + q + 1, :]

    def columns(ref, at, q):
        return ref[at, q * block : (q + 1) * block].astype(jnp.float32)

    def tile_rows(place, part):
        row_block = lax.rem(given_start + place, row_blocks)
        return pl.ds(pl.multiple_of(row_block * block + part * chunk, chunk), chunk)

    def change_at(place, part, slot):
        total = None
        if place < row_blocks - 1:
            at = pl.ds(place * block + part * chunk, chunk)
            total = pick(flags, 0, place) * columns(change, at, slot)
        if place > 0:
            at = pl.ds((place - 1) * block + part * chunk, chunk)
            term = pick(flags, row_blocks, place) * columns(change, at, slot)
            total = term if total is None else total + term
        return total

    def spread(flag_ref, start, slots):
        placed = []
        for q in range(col_blocks):
            total = None
            if q < col_blocks - 1:
                total = pick(flag_ref, start, q) * slots[q]
            if q > 0:
                term = pick(flag_ref, start + col_blocks, q) * slots[q - 1]
                total = term if total is None else total + term
            placed.append(total)
        return placed

    left_copy.wait()
    tile_copy.wait()
    swaps = []
    for place in range(row_blocks):
        for part in range(parts):
            if place < row_blocks - 1:
                unit = place * parts + part
                pump(unit + 1 + 1)
                lefts[unit].finish()
                at = pl.ds(unit * chunk, chunk)
                change[at, :] = jnp.dot(
                    left[at, :], product[...], preferred_element_type=jnp.float32
                )
            if place < half:
                at = pl.ds(place * block + part * chunk, chunk)
                rows_at = tile_rows(place, part)
                for slot in range(col_blocks - 1):
                    first = pick(flags, 16, slot)
                    kept = first * columns(tile, rows_at, slot)
                    kept = kept + (1.0 - first) * columns(tile, rows_at, slot + 1)
                    kept = kept - change_at(place, part, slot)
                    given[at, slot * block : (slot + 1) * block] = kept.astype(given.dtype)
                swap = pltpu.make_async_remote_copy(
                    src_ref=given.at[at, :],
                    dst_ref=received.at[at, :],
                    send_sem=swap_sems.at[0, len(swaps)],
                    recv_sem=swap_sems.at[1, len(swaps)],
                    device_id={"grid": partner},
                    device_id_type=MESH,
                )
                swap.start()
                swaps.append(swap)
            else:
                at = pl.ds((place - half) * block + part * chunk, chunk)
                rows_at = tile_rows(place, part)
                own = spread(
                    flags, 16, [change_at(place, part, c) for c in range(col_blocks - 1)]
                )
                if place == half and part == 0:
                    for copy in early:
                        copy.wait_recv()
                swaps[(place - half) * parts + part].wait_recv()
                other = spread(
                    other_flags, 0, [columns(received, at, c) for c in range(col_blocks - 1)]
                )
                for q in range(col_blocks):
                    kept = (columns(tile, rows_at, q) - own[q]).astype(jnp.bfloat16)
                    term = other[q] + pick(other_flags, 2 * col_blocks, q) * columns(raw, at, 0)
                    out_ref[at, q * block : (q + 1) * block] = (
                        kept.astype(jnp.float32) + term
                    ).astype(out_ref.dtype)
    for copy in early:
        copy.wait_send()
    for gather in [inv_col, product_all, upper_all] + lefts:
        gather.sent()
    for swap in swaps:
        swap.wait_send()


def cut_kernel(block, chosen, left_ref, upper_ref, left_out, upper_out, raw_out, flags_out):
    row_pos = lax.axis_index("row")
    col_pos = lax.axis_index("col")
    n_rows = lax.axis_size("row")
    row_blocks = left_ref.shape[0] // block
    col_blocks = upper_ref.shape[1] // block

    def is_listed(number):
        found = jnp.int32(0)
        for k in range(n_rows, chosen.shape[0]):
            found = found + (chosen[k] == number).astype(jnp.int32)
        return found.astype(jnp.float32)

    given_start = (1 - lax.rem(lax.axis_index("grid"), 2)) * (row_blocks // 2)
    own_row = lax.rem(chosen[row_pos], row_blocks)
    pivot_place = lax.rem(own_row + row_blocks - given_start, row_blocks)
    for slot in range(row_blocks - 1):
        place = slot + (slot >= pivot_place).astype(jnp.int32)
        row_block = lax.rem(given_start + place, row_blocks)
        values = left_ref[pl.ds(pl.multiple_of(row_block * block, block), block), :]
        kept = values.astype(jnp.float32) * is_listed(row_pos * row_blocks + row_block)
        left_out[pl.ds(slot * block, block), :] = kept.astype(left_out.dtype)
    raw_rows = row_blocks // 2 * block
    raw_out[...] = left_ref[pl.ds(pl.multiple_of(given_start * block, block), raw_rows), :]
    own_col = lax.rem(chosen[col_pos], col_blocks)
    for slot in range(col_blocks - 1):
        c = slot + (slot >= own_col).astype(jnp.int32)
        values = upper_ref[:, pl.ds(pl.multiple_of(c * block, block), block)]
        kept = values.astype(jnp.float32) * is_listed(col_pos * col_blocks + c)
        upper_out[:, slot * block : (slot + 1) * block] = kept.astype(upper_out.dtype)
    flags_out[...] = jnp.zeros_like(flags_out)
    rows_of = []
    for place in range(row_blocks):
        rows_of.append((place, pivot_place > place))
        rows_of.append((row_blocks + place, pivot_place < place))
    for q in range(col_blocks):
        rows_of.append((16 + q, own_col > q))
        rows_of.append((16 + col_blocks + q, own_col < q))
        rows_of.append((16 + 2 * col_blocks + q, own_col == q))
    for row, holds in rows_of:
        flags_out[row : row + 1, :] = jnp.full(
            (1, flags_out.shape[1]), holds.astype(jnp.int32).astype(jnp.float32)
        )


def first_level(tile, inverse, chosen, out_dtype):
    n_rows = lax.axis_size("row")
    n_cols = lax.axis_size("col")
    rows, cols = tile.shape
    width = inverse.shape[0]
    block = width // n_rows
    slots = rows // block - 1
    narrow = cols - block
    parts = 2
    bf16 = jnp.bfloat16
    dma = pltpu.SemaphoreType.DMA
    left, upper, raw, flags = pl.pallas_call(
        functools.partial(cut_kernel, block),
        grid_spec=pltpu.PrefetchScalarGridSpec(
            num_scalar_prefetch=1,
            grid=(1,),
            in_specs=[
                pl.BlockSpec(
                    (rows, block),
                    lambda i, chosen: (0, lax.rem(chosen[lax.axis_index("col")], cols // block)),
                ),
                pl.BlockSpec(
                    (block, cols),
                    lambda i, chosen: (lax.rem(chosen[lax.axis_index("row")], rows // block), 0),
                ),
            ],
            out_specs=[
                pl.BlockSpec((slots * block, block), lambda i, chosen: (0, 0)),
                pl.BlockSpec((block, narrow), lambda i, chosen: (0, 0)),
                pl.BlockSpec((rows // 2, block), lambda i, chosen: (0, 0)),
                pl.BlockSpec((32, block), lambda i, chosen: (0, 0)),
            ],
        ),
        out_shape=[
            jax.ShapeDtypeStruct((slots * block, block), bf16),
            jax.ShapeDtypeStruct((block, narrow), bf16),
            jax.ShapeDtypeStruct((rows // 2, block), bf16),
            jax.ShapeDtypeStruct((32, block), jnp.float32),
        ],
    )(chosen, tile, tile)
    return pl.pallas_call(
        functools.partial(eliminate_kernel, block, parts),
        out_shape=jax.ShapeDtypeStruct((rows // 2, cols), out_dtype),
        in_specs=[pl.BlockSpec(memory_space=pltpu.VMEM)] + [pl.BlockSpec(memory_space=pl.ANY)] * 5,
        out_specs=pl.BlockSpec(memory_space=pltpu.VMEM),
        scratch_shapes=[
            pltpu.VMEM((rows, cols), bf16),
            pltpu.VMEM((slots * block, width), bf16),
            pltpu.VMEM((width, narrow), bf16),
            pltpu.VMEM((block, width), bf16),
            pltpu.VMEM((width, narrow), bf16),
            pltpu.VMEM((slots * block, narrow), jnp.float32),
            pltpu.VMEM((rows // 2, narrow), bf16),
            pltpu.VMEM((rows // 2, narrow), bf16),
            pltpu.VMEM((rows // 2, block), bf16),
            pltpu.VMEM((16, block), jnp.float32),
            dma((4,)),
            dma((2, 2, n_cols - 1)),
            dma((2, n_rows - 1)),
            dma((2, n_rows - 1)),
            dma((2, slots * parts, 2, n_cols - 1)),
            dma((2, (slots + 1) // 2 * parts)),
            dma((2, 2)),
        ],
        compiler_params=pltpu.CompilerParams(
            collective_id=0, has_side_effects=True, vmem_limit_bytes=56 * 1024 * 1024
        ),
    )(flags, tile, left, upper, raw, inverse)


def shards(schur, d_inv, blocks):
    n_rows = lax.axis_size("row")
    grid_pos = lax.axis_index("grid")
    row_pos = lax.axis_index("row")
    col_pos = lax.axis_index("col")
    levels = blocks.shape[0]
    quarter_rows = schur.shape[1]
    local_cols = schur.shape[2]
    width = d_inv.shape[2]
    block = width // n_rows
    col_start = col_pos * local_cols
    col_ids = (col_start + jnp.arange(local_cols, dtype=jnp.int32)) // block
    current = first_level(
        schur[0], d_inv[0, 0], blocks[0, 0], jnp.bfloat16 if levels == 1 else jnp.float32
    )
    row_shift = (grid_pos & 1) * (quarter_rows // 2)
    for height in range(1, levels):
        rows_here = current.shape[0]
        count = rows_here // block
        chosen = blocks[height, 0]
        pivots = chosen[:n_rows]
        listed = chosen[n_rows:]
        row_start = row_pos * quarter_rows + row_shift
        col_keep = jnp.any(col_ids[:, None] == listed[None, :], axis=1)
        left_piece = lax.dynamic_slice_in_dim(
            current, pivots[col_pos] * block - col_start, block, 1
        ).astype(jnp.bfloat16)
        left_panel = lax.all_gather(left_piece, "col", axis=1, tiled=True)
        part = min(block, rows_here)
        offset = pivots[row_pos] * block - row_start
        upper_piece = jnp.zeros((block, local_cols), jnp.bfloat16)
        for start in range(0, block, part):
            inside = offset + start
            owned = (inside >= 0) & (inside < rows_here)
            rows_of = lax.dynamic_slice_in_dim(
                current, jnp.clip(inside, 0, rows_here - part), part, 0
            )
            upper_piece = lax.dynamic_update_slice_in_dim(
                upper_piece, jnp.where(owned, rows_of, 0.0).astype(jnp.bfloat16), start, 0
            )
        for member_bit in range(height):
            upper_piece = upper_piece + swapped(upper_piece, "grid", member_bit)
        upper_panel = lax.all_gather(upper_piece, "row", axis=0, tiled=True)
        upper_panel = jnp.where(col_keep[None, :], upper_panel, jnp.zeros((), jnp.bfloat16))
        inverse_full = lax.all_gather(d_inv[height, 0], "col", axis=1, tiled=True)

        def update_block(tile_rows, left_rows):
            scaled = jnp.dot(left_rows, inverse_full, preferred_element_type=jnp.float32).astype(
                jnp.bfloat16
            )
            return tile_rows - jnp.dot(scaled, upper_panel, preferred_element_type=jnp.float32)

        pieces = []
        for start in range(0, rows_here, part):
            row_id = (row_start + start) // block
            pieces.append(
                lax.cond(
                    jnp.any(row_id == listed),
                    update_block,
                    unchanged,
                    current[start : start + part],
                    left_panel[start : start + part],
                )
            )
        updated = jnp.concatenate(pieces, axis=0).astype(jnp.bfloat16)
        bit_value = grid_pos >> height & 1
        half_rows = rows_here // 2
        kept = lax.dynamic_slice_in_dim(updated, bit_value * half_rows, half_rows, 0)
        given = lax.dynamic_slice_in_dim(updated, (1 - bit_value) * half_rows, half_rows, 0)
        received = swapped(given, "grid", height)
        current = kept.astype(jnp.float32) + received.astype(jnp.float32)
        row_shift = row_shift + bit_value * half_rows
    return current.astype(jnp.bfloat16)[None]


def solution(mesh):
    return jax.shard_map(
        shards,
        mesh=mesh,
        in_specs=(P("grid", "row", "col"), P(None, "grid", None, "col"), P(None, "grid", None)),
        out_specs=P("grid", "row", "col"),
        check_vma=False,
    )
```

```python
import functools

import jax
import jax.numpy as jnp
from jax import lax
from jax.experimental import pallas as pl
from jax.experimental.pallas import tpu as pltpu
from jax.sharding import PartitionSpec as P

MESH = pl.DeviceIdType.MESH


def swapped(block, axis, apart):
    count = lax.axis_size(axis)
    route = []
    for low in range(count):
        high = low | 1 << apart
        if high != low and high < count:
            route += [(low, high), (high, low)]
    return lax.ppermute(block, axis, route)


def unchanged(tile_rows, other_rows):
    return tile_rows


def flipped(index, bits):
    bit = 1
    while bit <= bits:
        if bits & bit:
            index = index + bit - 2 * bit * lax.rem(lax.div(index, bit), 2)
        bit *= 2
    return index


class Gather:
    def __init__(self, axis, own, place, sems):
        self.count = lax.axis_size(axis)
        me = lax.axis_index(axis)
        self.copies = {}
        for s in range(1, self.count):
            low = s & -s
            rest = s ^ low
            held = flipped(me, rest)
            self.copies[s] = pltpu.make_async_remote_copy(
                src_ref=own if rest == 0 else place(held),
                dst_ref=place(held),
                send_sem=sems[0].at[s - 1],
                recv_sem=sems[1].at[s - 1],
                device_id={axis: flipped(me, low)},
                device_id_type=MESH,
            )
        self.waited = set()

    def start(self):
        for s in reversed(range(1, self.count)):
            if s & (s - 1) == 0:
                self.copies[s].start()

    def arrive(self, s):
        if s not in self.waited:
            self.waited.add(s)
            self.copies[s].wait_recv()

    def forward(self):
        for rest in reversed(range(2, self.count)):
            lows = [low for low in range(1, rest) if low & (low - 1) == 0 and low < (rest & -rest)]
            if lows:
                self.arrive(rest)
                for low in lows:
                    self.copies[rest | low].start()

    def finish(self):
        for s in range(1, self.count):
            self.arrive(s)

    def sent(self):
        for s in range(1, self.count):
            self.copies[s].wait_send()


class Relay:
    def __init__(self, axis, own, place, sems):
        self.count = lax.axis_size(axis)
        self.me = lax.axis_index(axis)
        self.copies = {}
        for side, step in enumerate((1, -1)):
            for d in range(self.count - 1):
                held = jnp.clip(self.me - step * d, 0, self.count - 1)
                self.copies[side, d] = pltpu.make_async_remote_copy(
                    src_ref=own if d == 0 else place(held),
                    dst_ref=place(held),
                    send_sem=sems[0].at[side, d],
                    recv_sem=sems[1].at[side, d],
                    device_id={axis: jnp.clip(self.me + step, 0, self.count - 1)},
                    device_id_type=MESH,
                )

    def sends(self, side, d):
        if side == 0:
            return (self.me >= d) & (self.me + 1 < self.count)
        return (self.me + d < self.count) & (self.me >= 1)

    def receives(self, side, d):
        if side == 0:
            return self.me >= d + 1
        return self.me + d + 1 < self.count

    def start(self):
        for side in range(2):
            pl.when(self.sends(side, 0))(self.copies[side, 0].start)

    def hop(self, d):
        for side in range(2):
            pl.when(self.receives(side, d))(self.copies[side, d].wait_recv)
            if d + 1 < self.count - 1:
                pl.when(self.sends(side, d + 1))(self.copies[side, d + 1].start)

    def forward(self):
        for d in range(self.count - 2):
            self.hop(d)

    def finish(self):
        self.hop(self.count - 2)

    def sent(self):
        for side in range(2):
            for d in range(self.count - 1):
                pl.when(self.sends(side, d))(self.copies[side, d].wait_send)


def eliminate_kernel(
    block,
    parts,
    flags,
    tile_ref,
    left_ref,
    upper_ref,
    raw_ref,
    inv_ref,
    out_ref,
    tile,
    left,
    upper,
    inv,
    product,
    change,
    given,
    received,
    raw,
    other_flags,
    local_sems,
    inv_col_sems,
    product_all_sems,
    upper_sems,
    left_sems,
    swap_sems,
    early_sems,
):
    row_pos = lax.axis_index("row")
    col_pos = lax.axis_index("col")
    grid_pos = lax.axis_index("grid")
    n_rows = lax.axis_size("row")
    n_cols = lax.axis_size("col")
    row_blocks = tile.shape[0] // block
    col_blocks = tile.shape[1] // block
    width = inv.shape[1]
    piece = inv_ref.shape[1]
    slab = width // n_rows
    chunk = block // parts
    half = row_blocks // 2
    bit_value = lax.rem(grid_pos, 2)
    partner = flipped(grid_pos, 1)

    inv_copy = pltpu.make_async_copy(
        inv_ref.at[pl.ds(row_pos * slab, slab), :],
        inv.at[:, pl.ds(pl.multiple_of(col_pos * piece, piece), piece)],
        local_sems.at[0],
    )
    tile_copy = pltpu.make_async_copy(tile_ref, tile, local_sems.at[1])
    upper_copy = pltpu.make_async_copy(
        upper_ref, upper.at[pl.ds(row_pos * slab, slab), :], local_sems.at[2]
    )
    left_copy = pltpu.make_async_copy(
        left_ref,
        left.at[:, pl.ds(pl.multiple_of(col_pos * piece, piece), piece)],
        local_sems.at[3],
    )
    for copy in (inv_copy, upper_copy, left_copy, tile_copy):
        copy.start()

    barrier = pltpu.get_barrier_semaphore()
    bit = 1
    while bit < n_rows:
        peer = {"row": flipped(row_pos, bit)}
        pl.semaphore_signal(barrier, inc=1, device_id=peer, device_id_type=MESH)
        bit *= 2
    pl.semaphore_signal(barrier, inc=1, device_id={"grid": partner}, device_id_type=MESH)
    for apart in range(1, n_cols):
        peer = {"col": lax.rem(col_pos + apart, n_cols)}
        pl.semaphore_signal(barrier, inc=1, device_id=peer, device_id_type=MESH)
    pl.semaphore_wait(barrier, n_rows.bit_length() + n_cols - 1)

    def inv_place(held):
        return inv.at[:, pl.ds(pl.multiple_of(held * piece, piece), piece)]

    def slab_place(held):
        return product.at[pl.ds(held * slab, slab), :]

    def upper_place(held):
        return upper.at[pl.ds(held * slab, slab), :]

    inv_col = Gather(
        "col",
        inv_ref.at[pl.ds(row_pos * slab, slab), :],
        inv_place,
        (inv_col_sems.at[0, 0], inv_col_sems.at[1, 0]),
    )
    product_all = Gather(
        "row", slab_place(row_pos), slab_place, (product_all_sems.at[0], product_all_sems.at[1])
    )
    upper_all = Gather(
        "row", upper_ref, upper_place, (upper_sems.at[0], upper_sems.at[1])
    )

    def left_gather(unit):
        def place(held):
            return left.at[
                pl.ds(unit * chunk, chunk), pl.ds(pl.multiple_of(held * piece, piece), piece)
            ]

        return Relay(
            "col",
            left_ref.at[pl.ds(unit * chunk, chunk), :],
            place,
            (left_sems.at[0, unit], left_sems.at[1, unit]),
        )

    lefts = [left_gather(unit) for unit in range((row_blocks - 1) * parts)]

    given_start = (1 - bit_value) * half

    inv_col.start()
    upper_all.start()
    early = [
        pltpu.make_async_remote_copy(
            src_ref=source,
            dst_ref=target,
            send_sem=early_sems.at[0, i],
            recv_sem=early_sems.at[1, i],
            device_id={"grid": partner},
            device_id_type=MESH,
        )
        for i, (source, target) in enumerate(
            ((raw_ref, raw), (flags.at[pl.ds(16, 16), :], other_flags))
        )
    ]
    for copy in early:
        copy.start()
    units = len(lefts)
    ahead = 2
    for unit in range(min(ahead, units)):
        lefts[unit].start()
    begun = min(ahead, units)
    inv_col.forward()
    passed = 0

    def pump(upto):
        nonlocal passed, begun
        while passed < min(upto, units):
            if begun < units:
                lefts[begun].start()
                begun += 1
            lefts[passed].forward()
            passed += 1

    upper_all.forward()
    inv_col.finish()
    inv_copy.wait()
    upper_all.finish()
    upper_copy.wait()
    product[pl.ds(row_pos * slab, slab), :] = jnp.dot(
        inv[...], upper[...], preferred_element_type=jnp.float32
    ).astype(jnp.bfloat16)
    product_all.start()
    pump(2)
    product_all.forward()
    pump(3)
    product_all.finish()

    def pick(flag_ref, start, q):
        return flag_ref[start + q : start + q + 1, :]

    def columns(ref, at, q):
        return ref[at, q * block : (q + 1) * block].astype(jnp.float32)

    def tile_rows(place, part):
        row_block = lax.rem(given_start + place, row_blocks)
        return pl.ds(pl.multiple_of(row_block * block + part * chunk, chunk), chunk)

    def change_at(place, part, slot):
        total = None
        if place < row_blocks - 1:
            at = pl.ds(place * block + part * chunk, chunk)
            total = pick(flags, 0, place) * columns(change, at, slot)
        if place > 0:
            at = pl.ds((place - 1) * block + part * chunk, chunk)
            term = pick(flags, row_blocks, place) * columns(change, at, slot)
            total = term if total is None else total + term
        return total

    def spread(flag_ref, start, slots):
        placed = []
        for q in range(col_blocks):
            total = None
            if q < col_blocks - 1:
                total = pick(flag_ref, start, q) * slots[q]
            if q > 0:
                term = pick(flag_ref, start + col_blocks, q) * slots[q - 1]
                total = term if total is None else total + term
            placed.append(total)
        return placed

    left_copy.wait()
    tile_copy.wait()
    swaps = []
    for place in range(row_blocks):
        for part in range(parts):
            if place < row_blocks - 1:
                unit = place * parts + part
                pump(unit + 1 + 1)
                lefts[unit].finish()
                at = pl.ds(unit * chunk, chunk)
                change[at, :] = jnp.dot(
                    left[at, :], product[...], preferred_element_type=jnp.float32
                )
            if place < half:
                at = pl.ds(place * block + part * chunk, chunk)
                rows_at = tile_rows(place, part)
                for slot in range(col_blocks - 1):
                    first = pick(flags, 16, slot)
                    kept = first * columns(tile, rows_at, slot)
                    kept = kept + (1.0 - first) * columns(tile, rows_at, slot + 1)
                    kept = kept - change_at(place, part, slot)
                    given[at, slot * block : (slot + 1) * block] = kept.astype(given.dtype)
                swap = pltpu.make_async_remote_copy(
                    src_ref=given.at[at, :],
                    dst_ref=received.at[at, :],
                    send_sem=swap_sems.at[0, len(swaps)],
                    recv_sem=swap_sems.at[1, len(swaps)],
                    device_id={"grid": partner},
                    device_id_type=MESH,
                )
                swap.start()
                swaps.append(swap)
            else:
                at = pl.ds((place - half) * block + part * chunk, chunk)
                rows_at = tile_rows(place, part)
                own = spread(
                    flags, 16, [change_at(place, part, c) for c in range(col_blocks - 1)]
                )
                if place == half and part == 0:
                    for copy in early:
                        copy.wait_recv()
                swaps[(place - half) * parts + part].wait_recv()
                other = spread(
                    other_flags, 0, [columns(received, at, c) for c in range(col_blocks - 1)]
                )
                for q in range(col_blocks):
                    kept = (columns(tile, rows_at, q) - own[q]).astype(jnp.bfloat16)
                    term = other[q] + pick(other_flags, 2 * col_blocks, q) * columns(raw, at, 0)
                    out_ref[at, q * block : (q + 1) * block] = (
                        kept.astype(jnp.float32) + term
                    ).astype(out_ref.dtype)
    for copy in early:
        copy.wait_send()
    for gather in [inv_col, product_all, upper_all] + lefts:
        gather.sent()
    for swap in swaps:
        swap.wait_send()


def cut_kernel(block, chosen, left_ref, upper_ref, left_out, upper_out, raw_out, flags_out):
    row_pos = lax.axis_index("row")
    col_pos = lax.axis_index("col")
    n_rows = lax.axis_size("row")
    row_blocks = left_ref.shape[0] // block
    col_blocks = upper_ref.shape[1] // block

    def is_listed(number):
        found = jnp.int32(0)
        for k in range(n_rows, chosen.shape[0]):
            found = found + (chosen[k] == number).astype(jnp.int32)
        return found.astype(jnp.float32)

    given_start = (1 - lax.rem(lax.axis_index("grid"), 2)) * (row_blocks // 2)
    own_row = lax.rem(chosen[row_pos], row_blocks)
    pivot_place = lax.rem(own_row + row_blocks - given_start, row_blocks)
    for slot in range(row_blocks - 1):
        place = slot + (slot >= pivot_place).astype(jnp.int32)
        row_block = lax.rem(given_start + place, row_blocks)
        values = left_ref[pl.ds(pl.multiple_of(row_block * block, block), block), :]
        kept = values.astype(jnp.float32) * is_listed(row_pos * row_blocks + row_block)
        left_out[pl.ds(slot * block, block), :] = kept.astype(left_out.dtype)
    raw_rows = row_blocks // 2 * block
    raw_out[...] = left_ref[pl.ds(pl.multiple_of(given_start * block, block), raw_rows), :]
    own_col = lax.rem(chosen[col_pos], col_blocks)
    for slot in range(col_blocks - 1):
        c = slot + (slot >= own_col).astype(jnp.int32)
        values = upper_ref[:, pl.ds(pl.multiple_of(c * block, block), block)]
        kept = values.astype(jnp.float32) * is_listed(col_pos * col_blocks + c)
        upper_out[:, slot * block : (slot + 1) * block] = kept.astype(upper_out.dtype)
    flags_out[...] = jnp.zeros_like(flags_out)
    rows_of = []
    for place in range(row_blocks):
        rows_of.append((place, pivot_place > place))
        rows_of.append((row_blocks + place, pivot_place < place))
    for q in range(col_blocks):
        rows_of.append((16 + q, own_col > q))
        rows_of.append((16 + col_blocks + q, own_col < q))
        rows_of.append((16 + 2 * col_blocks + q, own_col == q))
    for row, holds in rows_of:
        flags_out[row : row + 1, :] = jnp.full(
            (1, flags_out.shape[1]), holds.astype(jnp.int32).astype(jnp.float32)
        )


def first_level(tile, inverse, chosen, out_dtype):
    n_rows = lax.axis_size("row")
    n_cols = lax.axis_size("col")
    rows, cols = tile.shape
    width = inverse.shape[0]
    block = width // n_rows
    slots = rows // block - 1
    narrow = cols - block
    parts = 2
    bf16 = jnp.bfloat16
    dma = pltpu.SemaphoreType.DMA
    left, upper, raw, flags = pl.pallas_call(
        functools.partial(cut_kernel, block),
        grid_spec=pltpu.PrefetchScalarGridSpec(
            num_scalar_prefetch=1,
            grid=(1,),
            in_specs=[
                pl.BlockSpec(
                    (rows, block),
                    lambda i, chosen: (0, lax.rem(chosen[lax.axis_index("col")], cols // block)),
                ),
                pl.BlockSpec(
                    (block, cols),
                    lambda i, chosen: (lax.rem(chosen[lax.axis_index("row")], rows // block), 0),
                ),
            ],
            out_specs=[
                pl.BlockSpec((slots * block, block), lambda i, chosen: (0, 0)),
                pl.BlockSpec((block, narrow), lambda i, chosen: (0, 0)),
                pl.BlockSpec((rows // 2, block), lambda i, chosen: (0, 0)),
                pl.BlockSpec((32, block), lambda i, chosen: (0, 0)),
            ],
        ),
        out_shape=[
            jax.ShapeDtypeStruct((slots * block, block), bf16),
            jax.ShapeDtypeStruct((block, narrow), bf16),
            jax.ShapeDtypeStruct((rows // 2, block), bf16),
            jax.ShapeDtypeStruct((32, block), jnp.float32),
        ],
    )(chosen, tile, tile)
    return pl.pallas_call(
        functools.partial(eliminate_kernel, block, parts),
        out_shape=jax.ShapeDtypeStruct((rows // 2, cols), out_dtype),
        in_specs=[pl.BlockSpec(memory_space=pltpu.VMEM)] + [pl.BlockSpec(memory_space=pl.ANY)] * 5,
        out_specs=pl.BlockSpec(memory_space=pltpu.VMEM),
        scratch_shapes=[
            pltpu.VMEM((rows, cols), bf16),
            pltpu.VMEM((slots * block, width), bf16),
            pltpu.VMEM((width, narrow), bf16),
            pltpu.VMEM((block, width), bf16),
            pltpu.VMEM((width, narrow), bf16),
            pltpu.VMEM((slots * block, narrow), jnp.float32),
            pltpu.VMEM((rows // 2, narrow), bf16),
            pltpu.VMEM((rows // 2, narrow), bf16),
            pltpu.VMEM((rows // 2, block), bf16),
            pltpu.VMEM((16, block), jnp.float32),
            dma((4,)),
            dma((2, 2, n_cols - 1)),
            dma((2, n_rows - 1)),
            dma((2, n_rows - 1)),
            dma((2, slots * parts, 2, n_cols - 1)),
            dma((2, (slots + 1) // 2 * parts)),
            dma((2, 2)),
        ],
        compiler_params=pltpu.CompilerParams(
            collective_id=0, has_side_effects=True, vmem_limit_bytes=56 * 1024 * 1024
        ),
    )(flags, tile, left, upper, raw, inverse)


def shards(schur, d_inv, blocks):
    n_rows = lax.axis_size("row")
    grid_pos = lax.axis_index("grid")
    row_pos = lax.axis_index("row")
    col_pos = lax.axis_index("col")
    levels = blocks.shape[0]
    quarter_rows = schur.shape[1]
    local_cols = schur.shape[2]
    width = d_inv.shape[2]
    block = width // n_rows
    col_start = col_pos * local_cols
    col_ids = (col_start + jnp.arange(local_cols, dtype=jnp.int32)) // block
    current = first_level(
        schur[0], d_inv[0, 0], blocks[0, 0], jnp.bfloat16 if levels == 1 else jnp.float32
    )
    row_shift = (grid_pos & 1) * (quarter_rows // 2)
    for height in range(1, levels):
        rows_here = current.shape[0]
        count = rows_here // block
        chosen = blocks[height, 0]
        pivots = chosen[:n_rows]
        listed = chosen[n_rows:]
        row_start = row_pos * quarter_rows + row_shift
        col_keep = jnp.any(col_ids[:, None] == listed[None, :], axis=1)
        left_piece = lax.dynamic_slice_in_dim(
            current, pivots[col_pos] * block - col_start, block, 1
        ).astype(jnp.bfloat16)
        left_panel = lax.all_gather(left_piece, "col", axis=1, tiled=True)
        part = min(block, rows_here)
        offset = pivots[row_pos] * block - row_start
        upper_piece = jnp.zeros((block, local_cols), jnp.bfloat16)
        for start in range(0, block, part):
            inside = offset + start
            owned = (inside >= 0) & (inside < rows_here)
            rows_of = lax.dynamic_slice_in_dim(
                current, jnp.clip(inside, 0, rows_here - part), part, 0
            )
            upper_piece = lax.dynamic_update_slice_in_dim(
                upper_piece, jnp.where(owned, rows_of, 0.0).astype(jnp.bfloat16), start, 0
            )
        for member_bit in range(height):
            upper_piece = upper_piece + swapped(upper_piece, "grid", member_bit)
        upper_panel = lax.all_gather(upper_piece, "row", axis=0, tiled=True)
        upper_panel = jnp.where(col_keep[None, :], upper_panel, jnp.zeros((), jnp.bfloat16))
        inverse_full = lax.all_gather(d_inv[height, 0], "col", axis=1, tiled=True)

        def update_block(tile_rows, left_rows):
            scaled = jnp.dot(left_rows, inverse_full, preferred_element_type=jnp.float32).astype(
                jnp.bfloat16
            )
            return tile_rows - jnp.dot(scaled, upper_panel, preferred_element_type=jnp.float32)

        pieces = []
        for start in range(0, rows_here, part):
            row_id = (row_start + start) // block
            pieces.append(
                lax.cond(
                    jnp.any(row_id == listed),
                    update_block,
                    unchanged,
                    current[start : start + part],
                    left_panel[start : start + part],
                )
            )
        updated = jnp.concatenate(pieces, axis=0).astype(jnp.bfloat16)
        bit_value = grid_pos >> height & 1
        half_rows = rows_here // 2
        kept = lax.dynamic_slice_in_dim(updated, bit_value * half_rows, half_rows, 0)
        given = lax.dynamic_slice_in_dim(updated, (1 - bit_value) * half_rows, half_rows, 0)
        received = swapped(given, "grid", height)
        current = kept.astype(jnp.float32) + received.astype(jnp.float32)
        row_shift = row_shift + bit_value * half_rows
    return current.astype(jnp.bfloat16)[None]


def solution(mesh):
    return jax.shard_map(
        shards,
        mesh=mesh,
        in_specs=(P("grid", "row", "col"), P(None, "grid", None, "col"), P(None, "grid", None)),
        out_specs=P("grid", "row", "col"),
        check_vma=False,
    )
```
